128 devices in a mesh: row: 8 (over y_lo, z), col: 16 (over x, y_hi, core).
Axes of the slice: x: 4, y: 4 (y_hi: 2, y_lo: 2; y = y_hi * 2 + y_lo), z: 4, core: 2. Of those that a mesh axis runs over, the one named last changes fastest.
Arguments:
- rhs: bfloat16 [8, 16, 128, 1024], P('row', 'col'), may hold values from -6 to 6
- operators: bfloat16 [8, 16, 3, 1024, 1024], P('row', 'col'), may hold values from -0.09375 to 0.09375
- positions: int32 [128], replicated, may hold values from 0 to 131071
- start_tick: int32 [128], replicated, may hold values from 0 to 7
Outputs:
- traces: bfloat16 [8, 16, 128, 1024], P('row', 'col')
The draws below stay inside these ranges and needn't reach their ends.
All inputs are finite; a program needn't handle non-finite values.
Results may differ from the reference program's by a relative error of at most 0.006.
Values may be sent and summed in bfloat16 or wider, within the bound.
A program may use at most 64 MiB of HBM per device.

```python
import jax
import jax.numpy as jnp
from jax import lax

TRACE = 1024
BATCH = 128
TICKS = 8
TURN = 4
POINTS = 131072
N_ROW = 8
N_COL = 16


def set_ends(array, own_key, smallest, high):
    extent = array.shape
    place = [jax.random.randint(jax.random.fold_in(own_key, axis), (), 0, extent[axis]) for axis in range(len(extent))]
    array = array.at[tuple(place)].set(smallest)
    longest = extent.index(max(extent))
    place[longest] = (place[longest] + 1) % extent[longest]
    return array.at[tuple(place)].set(high)


def block_scale(own_key, extent, cuts, least, top_value):
    gain, own = 1.0, jax.random.fold_in(own_key, 6)
    for position, blocks in cuts:
        draws = jnp.exp(jax.random.uniform(jax.random.fold_in(own, position), (blocks,), jnp.float32, least / len(cuts), top_value / len(cuts)))
        gain = gain * jnp.repeat(draws, extent[position] // blocks).reshape([-1 if axis == position else 1 for axis in range(len(extent))])
    return gain


def bell_draw(own_key, shape, scale, most, split=(), kind=jnp.bfloat16):
    array = jax.random.normal(own_key, shape, jnp.float32) * scale
    if len(split) > 0:
        array = block_scale(own_key, shape, split, -0.22, 0.18) * array
    return jnp.clip(array, min=-most, max=most).astype(kind)


def setup_inputs(seed: int = 0) -> dict:
    key_list = jax.random.split(jax.random.key(seed), 5)
    rhs = bell_draw(key_list[0], (N_ROW, N_COL, BATCH, TRACE), 1.0, 6.0, ((0, 8), (1, 16)))
    operators = bell_draw(key_list[1], (N_ROW, N_COL, 3, TRACE, TRACE), (4 * TRACE) ** -0.5, 0.09375, ((0, 8), (1, 16)))
    positions = set_ends(jax.random.randint(key_list[2], (BATCH,), 0, POINTS), jax.random.fold_in(key_list[2], 1), 0, POINTS - 1).astype(jnp.int32)
    start_tick = set_ends(jax.random.randint(key_list[3], (BATCH,), 0, TICKS), jax.random.fold_in(key_list[3], 1), 0, TICKS - 1).astype(jnp.int32)
    return dict(rhs=rhs, operators=operators, positions=positions, start_tick=start_tick)


def move_rows(field, sign):
    blank = jnp.zeros_like(field[:1])
    if sign > 0:
        return jnp.concatenate([blank, field[:-1]], axis=0)
    return jnp.concatenate([field[1:], blank], axis=0)


def move_cols(field, sign):
    blank = jnp.zeros_like(field[:, :1])
    if sign > 0:
        return jnp.concatenate([blank, field[:, :-1]], axis=1)
    return jnp.concatenate([field[:, 1:], blank], axis=1)


def reference(rhs, operators, positions, start_tick):
    n_sub = N_ROW * N_COL
    flat_ops = operators.reshape(n_sub, 3, TRACE, TRACE)
    subdomain = lax.broadcasted_iota(jnp.int32, (n_sub, BATCH, TRACE), 0)
    unknown = lax.broadcasted_iota(jnp.int32, (n_sub, BATCH, TRACE), 2)
    target = (subdomain * TRACE + unknown) == positions.astype(jnp.int32)[None, :, None]
    source = rhs.reshape(n_sub, BATCH, TRACE).astype(jnp.float32) + 4.0 * target.astype(jnp.float32)
    traces = jnp.zeros((N_ROW, N_COL, BATCH, TRACE), jnp.bfloat16)

    def combine(pack):
        incoming, mats = pack
        summed = jnp.dot(incoming[0], mats[0], preferred_element_type=jnp.float32)
        summed = summed + jnp.dot(incoming[1], mats[1], preferred_element_type=jnp.float32)
        return summed + jnp.dot(incoming[2], mats[2], preferred_element_type=jnp.float32)

    for tick_index in range(TICKS):
        sign = 1 if tick_index < TURN else -1
        if tick_index == 0:
            summed = source
        else:
            from_row = move_rows(traces, sign)
            from_col = move_cols(traces, sign)
            diagonal_in = move_cols(from_row, sign)
            stacked = jnp.stack([from_row, from_col, diagonal_in], axis=2).reshape(n_sub, 3, BATCH, TRACE)
            summed = source + lax.map(combine, (stacked, flat_ops))
        running = (tick_index >= start_tick)[None, :, None]
        traces = jnp.where(running, summed, 0.0).astype(jnp.bfloat16).reshape(N_ROW, N_COL, BATCH, TRACE)
    return traces
```

```python
import functools

import jax
import jax.numpy as jnp
from jax import lax
from jax.experimental import pallas as pl
from jax.experimental.pallas import tpu as pltpu
from jax.sharding import PartitionSpec as P

TICKS = 8
TURN = 4
GROUPS = (32, 32, 32, 32)
DIRECT_ON = True
DIRECT_OFF = False
VIA = (0, 1, 2, 3)
HALF = 4
LAG = 0


def sweep_kernel(
    rhs_ref, ops_hbm, pos_ref, start_ref, out_ref,
    ops, traces, up, left, corner, via, source, start, acc,
    op_sem, up_send, up_recv, left_send, left_recv, cor_send, cor_recv,
    via_send, via_recv, pass_send,
):
    row, col = lax.axis_index("row"), lax.axis_index("col")
    rows, cols = lax.axis_size("row"), lax.axis_size("col")
    batches, width = rhs_ref.shape
    last = TICKS - 1

    def op_copy(n):
        return pltpu.make_async_copy(ops_hbm.at[n], ops.at[n], op_sem.at[n])

    for n in range(3):
        op_copy(n).start()

    def in_rows(r):
        return jnp.logical_and(r >= 0, r < rows)

    def in_cols(c):
        return jnp.logical_and(c >= 0, c < cols)

    partners = [(-1, 0), (1, 0), (0, -1), (0, 1)]
    if DIRECT_ON or DIRECT_OFF:
        partners += [(-1, -1), (1, 1)]
    slot = lax.rem(row, HALF)
    is_end = jnp.logical_or(slot == 0, slot == HALF - 1)
    other_end = jnp.where(slot == 0, row + HALF - 1, row - (HALF - 1))
    other_half = lax.rem(row + HALF, 2 * HALF)

    barrier = pltpu.get_barrier_semaphore()

    def greet(r, c):
        pl.semaphore_signal(barrier, inc=1, device_id={"row": r, "col": c})

    for dr, dc in partners:
        @pl.when(jnp.logical_and(in_rows(row + dr), in_cols(col + dc)))
        def _(dr=dr, dc=dc):
            greet(row + dr, col + dc)

    @pl.when(is_end)
    def _():
        greet(other_end, col)
        greet(other_half, col)

    pos = jnp.broadcast_to(pos_ref[...], (batches, batches)).T
    first = jnp.broadcast_to(start_ref[...], (batches, batches)).T
    start[...] = first
    own = pos - (row * cols + col) * width
    lane = lax.broadcasted_iota(jnp.int32, (batches, batches), 1)
    for c in range(width // batches):
        cut = pl.ds(c * batches, batches)
        spike = jnp.where(own == lane + c * batches, 4.0, 0.0)
        value = rhs_ref[:, cut].astype(jnp.float32) + spike
        source[:, cut] = value
        traces[1, :, cut] = jnp.where(first <= 0, value, 0.0).astype(jnp.bfloat16)

    def sign_of(k):
        return jnp.where(k < TURN, 1, -1)

    def on_chip(c, s):
        return lax.rem(c, 2) == jnp.where(s > 0, 0, 1)

    def direct(c, s):
        on = on_chip(c, s)
        return jnp.logical_or(
            jnp.logical_and(on, DIRECT_ON), jnp.logical_and(jnp.logical_not(on), DIRECT_OFF)
        )

    bounds = []
    at = 0
    for size in GROUPS:
        bounds.append((at, size))
        at += size

    def remote(src, dst, send, recv, r, c):
        return pltpu.make_async_remote_copy(
            src, dst, send, recv, device_id={"row": r, "col": c},
            device_id_type=pl.DeviceIdType.MESH,
        )

    def up_copy(k, g, s):
        a, n = bounds[g]
        return remote(traces.at[k, pl.ds(a, n)], up.at[k, pl.ds(a, n)],
                      up_send.at[k, g], up_recv.at[k, g], row + s, col)

    def left_copy(k, g, s):
        a, n = bounds[g]
        return remote(traces.at[k, pl.ds(a, n)], left.at[k, pl.ds(a, n)],
                      left_send.at[k, g], left_recv.at[k, g], row, col + s)

    def diag_copy(k, g, s):
        a, n = bounds[g]
        return remote(traces.at[k, pl.ds(a, n)], corner.at[k, pl.ds(a, n)],
                      cor_send.at[k, g], cor_recv.at[k, g], row + s, col + s)

    def relay_copy(k, g, s):
        a, n = bounds[g]
        return remote(up.at[k, pl.ds(a, n)], corner.at[k, pl.ds(a, n)],
                      cor_send.at[k, g], cor_recv.at[k, g], row, col + s)

    def via_copy(k, g, s):
        a, n = bounds[g]
        return remote(traces.at[k, pl.ds(a, n)], via.at[k, pl.ds(a, n)],
                      via_send.at[k, g], via_recv.at[k, g], other_end, col)

    def pass_copy(k, g, s):
        a, n = bounds[g]
        return remote(via.at[k, pl.ds(a, n)], up.at[k, pl.ds(a, n)],
                      pass_send.at[k, g], up_recv.at[k, g], other_half, col)

    def crosses(s):
        return row == jnp.where(s > 0, HALF - 1, HALF)

    def passes(s):
        return row == jnp.where(s > 0, 0, 2 * HALF - 1)

    def up_direct(g, s):
        to_row = in_rows(row + s)
        if g in VIA:
            to_row = jnp.logical_and(to_row, jnp.logical_not(crosses(s)))
        return to_row

    def sends(k, s):
        to_row, to_col = in_rows(row + s), in_cols(col + s)
        from_row = in_rows(row - s)
        straight = direct(col, s)
        to_diag = jnp.logical_and(jnp.logical_and(to_row, to_col), straight)
        to_relay = jnp.logical_and(jnp.logical_and(from_row, to_col), jnp.logical_not(straight))
        return to_row, to_col, to_diag, to_relay

    def send(k, g):
        s = sign_of(k)
        to_row, to_col, to_diag, _ = sends(k, s)
        pl.when(up_direct(g, s))(lambda: up_copy(k, g, s).start())
        if g in VIA:
            pl.when(crosses(s))(lambda: via_copy(k, g, s).start())
        if DIRECT_ON or DIRECT_OFF:
            pl.when(to_diag)(lambda: diag_copy(k, g, s).start())
        pl.when(to_col)(lambda: left_copy(k, g, s).start())

    peers = jnp.where(is_end, 2, 0)
    for dr, dc in partners:
        peers += jnp.where(jnp.logical_and(in_rows(row + dr), in_cols(col + dc)), 1, 0)
    pl.semaphore_wait(barrier, peers)

    for g in range(len(GROUPS)):
        send(1, g)
    for n in range(3):
        op_copy(n).wait()

    def tick(k, carry):
        s = sign_of(k)
        _, _, _, to_relay = sends(k, s)
        has_up, has_left = in_rows(row - s), in_cols(col - s)
        has_corner = jnp.logical_and(has_up, has_left)
        def straight_part(g):
            a, n = bounds[g]
            here = pl.ds(a, n)
            if g in VIA:
                @pl.when(passes(s))
                def _():
                    via_copy(k, g, s).wait_recv()
                    pass_copy(k, g, s).start()

            acc[here] = source[here]

            @pl.when(has_up)
            def _():
                up_copy(k, g, s).wait_recv()
                pl.when(to_relay)(lambda: relay_copy(k, g, s).start())
                acc[here] += jnp.dot(up[k, here], ops[0], preferred_element_type=jnp.float32)

            @pl.when(has_left)
            def _():
                left_copy(k, g, s).wait_recv()
                acc[here] += jnp.dot(left[k, here], ops[1], preferred_element_type=jnp.float32)

        def corner_part(g):
            a, n = bounds[g]
            here = pl.ds(a, n)

            @pl.when(has_corner)
            def _():
                diag_copy(k, g, s).wait_recv()
                acc[here] += jnp.dot(corner[k, here], ops[2], preferred_element_type=jnp.float32)

            for c in range(width // batches):
                cut = pl.ds(c * batches, batches)
                traces[k + 1, here, cut] = jnp.where(
                    start[here] <= k, acc[here, cut], 0.0
                ).astype(jnp.bfloat16)

            @pl.when(k < last)
            def _():
                send(k + 1, g)

        for g in range(len(GROUPS) + LAG):
            if g < len(GROUPS):
                straight_part(g)
            if g >= LAG:
                corner_part(g - LAG)
        return carry

    lax.fori_loop(1, TICKS, tick, 0)
    out_ref[...] = traces[TICKS]

    def drain(k, carry):
        s = sign_of(k)
        to_row, to_col, to_diag, to_relay = sends(k, s)
        for g in range(len(GROUPS)):
            pl.when(up_direct(g, s))(lambda: up_copy(k, g, s).wait_send())
            if g in VIA:
                pl.when(crosses(s))(lambda: via_copy(k, g, s).wait_send())
                pl.when(passes(s))(lambda: pass_copy(k, g, s).wait_send())
            pl.when(to_col)(lambda: left_copy(k, g, s).wait_send())
            pl.when(jnp.logical_or(to_diag, to_relay))(lambda: diag_copy(k, g, s).wait_send())
        return carry

    lax.fori_loop(1, TICKS, drain, 0)


def body(rhs, operators, positions, start_tick):
    batches, width = rhs.shape[2:]
    n = len(GROUPS)
    sems = pltpu.SemaphoreType.DMA((TICKS, n))
    slots = pltpu.VMEM((TICKS, batches, width), jnp.bfloat16)
    vmem = pl.BlockSpec(memory_space=pltpu.VMEM)
    out = pl.pallas_call(
        sweep_kernel,
        out_shape=jax.ShapeDtypeStruct((batches, width), jnp.bfloat16),
        in_specs=[vmem, pl.BlockSpec(memory_space=pl.ANY), vmem, vmem],
        out_specs=vmem,
        scratch_shapes=[
            pltpu.VMEM((3, width, width), jnp.bfloat16),
            pltpu.VMEM((TICKS + 1, batches, width), jnp.bfloat16),
            slots, slots, slots, slots,
            pltpu.VMEM((batches, width), jnp.float32),
            pltpu.VMEM((batches, batches), jnp.int32),
            pltpu.VMEM((batches, width), jnp.float32),
            pltpu.SemaphoreType.DMA((3,)),
            sems, sems, sems, sems, sems, sems, sems, sems, sems,
        ],
        compiler_params=pltpu.CompilerParams(
            collective_id=0, has_side_effects=True, vmem_limit_bytes=40 << 20
        ),
    )(rhs[0, 0], operators[0, 0], positions[None], start_tick[None])
    return out[None, None]


def solution(mesh):
    placed = (P("row", "col", None, None), P("row", "col", None, None, None), P(), P())
    return jax.shard_map(
        body, mesh=mesh, in_specs=placed, out_specs=P("row", "col", None, None), check_vma=False
    )
```

```python
import functools

import jax
import jax.numpy as jnp
from jax import lax
from jax.experimental import pallas as pl
from jax.experimental.pallas import tpu as pltpu
from jax.sharding import PartitionSpec as P

TICKS = 8
TURN = 4
GROUPS = (32,)*4
DIRECT_ON = ()
DIRECT_OFF = ()
VIA = (0,1,3)
HALF = 4
ORDER = (('take', (0,)), ('late', (3,)), ('take', (1,)), ('dot', (0, 1)), ('end', (0,)), ('take', (2,)), ('end', (1,)), ('take', (3,)), ('dot', (2, 3)), ('end', (2,)))


def sweep_kernel(
    rhs_hbm, ops_hbm, pos_hbm, start_hbm, out_ref,
    rhs_ref, pos_ref, start_ref, ops, traces, up, left, corner, via, source, start, acc,
    in_sem, op_sem, up_send, up_recv, left_send, left_recv, cor_send, cor_recv,
    via_send, via_recv, pass_send, turn_send, diag_send,
):
    row, col = lax.axis_index("row"), lax.axis_index("col")
    rows, cols = lax.axis_size("row"), lax.axis_size("col")
    batches, width = rhs_hbm.shape
    last = TICKS - 1

    def op_copy(n):
        return pltpu.make_async_copy(ops_hbm.at[n], ops.at[n], op_sem.at[n])

    small = [
        pltpu.make_async_copy(there, here, in_sem.at[n])
        for n, (there, here) in enumerate(
            ((rhs_hbm, rhs_ref), (pos_hbm, pos_ref), (start_hbm, start_ref))
        )
    ]

    def in_rows(r):
        return jnp.logical_and(r >= 0, r < rows)

    def in_cols(c):
        return jnp.logical_and(c >= 0, c < cols)

    partners = [(-1, 0), (1, 0), (0, -1), (0, 1)]
    partners += [(-1, -1), (1, 1)]
    slot = lax.rem(row, HALF)
    is_end = jnp.logical_or(slot == 0, slot == HALF - 1)
    other_end = jnp.where(slot == 0, row + HALF - 1, row - (HALF - 1))
    other_half = lax.rem(row + HALF, 2 * HALF)
    beside = col + jnp.where(row < HALF, 1, -1)

    barrier = pltpu.get_barrier_semaphore()

    def greet(r, c):
        pl.semaphore_signal(barrier, inc=1, device_id={"row": r, "col": c})

    for dr, dc in partners:
        @pl.when(jnp.logical_and(in_rows(row + dr), in_cols(col + dc)))
        def _(dr=dr, dc=dc):
            greet(row + dr, col + dc)

    @pl.when(is_end)
    def _():
        greet(other_end, col)
        greet(other_half, col)

    @pl.when(jnp.logical_and(is_end, in_cols(beside)))
    def _():
        greet(other_half, beside)

    for copy in small:
        copy.start()
    for n in range(3):
        op_copy(n).start()
    for copy in small:
        copy.wait()

    pos = jnp.broadcast_to(pos_ref[...], (batches, batches)).T
    first = jnp.broadcast_to(start_ref[...], (batches, batches)).T
    start[...] = first
    own = pos - (row * cols + col) * width
    lane = lax.broadcasted_iota(jnp.int32, (batches, batches), 1)
    for c in range(width // batches):
        cut = pl.ds(c * batches, batches)
        spike = jnp.where(own == lane + c * batches, 4.0, 0.0)
        value = rhs_ref[:, cut].astype(jnp.float32) + spike
        source[:, cut] = value
        traces[1, :, cut] = jnp.where(first <= 0, value, 0.0).astype(jnp.bfloat16)

    def sign_of(k):
        return jnp.where(k < TURN, 1, -1)

    def on_chip(c, s):
        return lax.rem(c, 2) == jnp.where(s > 0, 0, 1)

    def direct(c, s, g):
        on = on_chip(c, s)
        return jnp.logical_or(
            jnp.logical_and(on, g in DIRECT_ON), jnp.logical_and(jnp.logical_not(on), g in DIRECT_OFF)
        )

    bounds = []
    at = 0
    for size in GROUPS:
        bounds.append((at, size))
        at += size

    def remote(src, dst, send, recv, r, c):
        return pltpu.make_async_remote_copy(
            src, dst, send, recv, device_id={"row": r, "col": c},
            device_id_type=pl.DeviceIdType.MESH,
        )

    def up_copy(k, g, s):
        a, n = bounds[g]
        return remote(traces.at[k, pl.ds(a, n)], up.at[k, pl.ds(a, n)],
                      up_send.at[k, g], up_recv.at[k, g], row + s, col)

    def left_copy(k, g, s):
        a, n = bounds[g]
        return remote(traces.at[k, pl.ds(a, n)], left.at[k, pl.ds(a, n)],
                      left_send.at[k, g], left_recv.at[k, g], row, col + s)

    def diag_copy(k, g, s):
        a, n = bounds[g]
        return remote(traces.at[k, pl.ds(a, n)], corner.at[k, pl.ds(a, n)],
                      diag_send.at[k, g], cor_recv.at[k, g], row + s, col + s)

    def relay_copy(k, g, s):
        a, n = bounds[g]
        return remote(up.at[k, pl.ds(a, n)], corner.at[k, pl.ds(a, n)],
                      cor_send.at[k, g], cor_recv.at[k, g], row, col + s)

    def via_copy(k, g, s):
        a, n = bounds[g]
        return remote(traces.at[k, pl.ds(a, n)], via.at[k, pl.ds(a, n)],
                      via_send.at[k, g], via_recv.at[k, g], other_end, col)

    def pass_copy(k, g, s):
        a, n = bounds[g]
        return remote(via.at[k, pl.ds(a, n)], up.at[k, pl.ds(a, n)],
                      pass_send.at[k, g], up_recv.at[k, g], other_half, col)

    def turn_copy(k, g, s):
        a, n = bounds[g]
        return remote(via.at[k, pl.ds(a, n)], corner.at[k, pl.ds(a, n)],
                      turn_send.at[k, g], cor_recv.at[k, g], other_half, col + s)

    def both(a, b):
        return jnp.logical_and(a, b)

    def crosses(s):
        return row == jnp.where(s > 0, HALF - 1, HALF)

    def enters(s):
        return row == jnp.where(s > 0, HALF, HALF - 1)

    def passes(s):
        return row == jnp.where(s > 0, 0, 2 * HALF - 1)

    def routes(g, s):
        to_row, to_col, from_row = in_rows(row + s), in_cols(col + s), in_rows(row - s)
        straight = direct(col, s, g)
        off = jnp.logical_not(on_chip(col, s))
        to_diag = straight
        if g in VIA:
            to_row_now = both(to_row, jnp.logical_not(crosses(s)))
            to_diag = both(to_diag, jnp.logical_not(both(off, crosses(s))))
        else:
            to_row_now = to_row
            to_diag = jnp.logical_or(to_diag, both(off, crosses(s)))
        bent = both(off, enters(s))
        return dict(
            up=to_row_now,
            left=to_col,
            diag=both(both(to_row, to_col), to_diag),
            relay=both(both(from_row, to_col), jnp.logical_not(jnp.logical_or(straight, bent))),
            via=crosses(s) if g in VIA else None,
            passed=passes(s) if g in VIA else None,
            turned=both(both(passes(s), to_col), off) if g in VIA else None,
        )

    def send(k, g):
        s = sign_of(k)
        route = routes(g, s)
        pl.when(route["up"])(lambda: up_copy(k, g, s).start())
        if g in VIA:
            pl.when(route["via"])(lambda: via_copy(k, g, s).start())
        pl.when(route["diag"])(lambda: diag_copy(k, g, s).start())
        pl.when(route["left"])(lambda: left_copy(k, g, s).start())

    peers = jnp.where(is_end, 2, 0) + jnp.where(jnp.logical_and(is_end, in_cols(beside)), 1, 0)
    for dr, dc in partners:
        peers += jnp.where(jnp.logical_and(in_rows(row + dr), in_cols(col + dc)), 1, 0)
    pl.semaphore_wait(barrier, peers)

    for g in range(len(GROUPS)):
        send(1, g)
    for n in range(3):
        op_copy(n).wait()

    def joined(groups):
        first, size = bounds[groups[0]][0], sum(bounds[g][1] for g in groups)
        return pl.ds(first, size)

    def pass_on(k, groups):
        s = sign_of(k)
        for g in groups:
            route = routes(g, s)
            if g in VIA:
                @pl.when(route["passed"])
                def _(g=g, route=route):
                    via_copy(k, g, s).wait_recv()
                    pl.when(route["turned"])(lambda: turn_copy(k, g, s).start())
                    pass_copy(k, g, s).start()

            @pl.when(in_rows(row - s))
            def _(g=g, route=route):
                up_copy(k, g, s).wait_recv()
                pl.when(route["relay"])(lambda: relay_copy(k, g, s).start())

    def straight_part(k, groups):
        s = sign_of(k)
        here = joined(groups)
        acc[here] = source[here]

        @pl.when(in_cols(col - s))
        def _():
            for g in groups:
                left_copy(k, g, s).wait_recv()
            acc[here] += jnp.dot(left[k, here], ops[1], preferred_element_type=jnp.float32)

        @pl.when(in_rows(row - s))
        def _():
            acc[here] += jnp.dot(up[k, here], ops[0], preferred_element_type=jnp.float32)

    def corner_part(k, groups):
        s = sign_of(k)
        here = joined(groups)

        @pl.when(jnp.logical_and(in_rows(row - s), in_cols(col - s)))
        def _():
            for g in groups:
                diag_copy(k, g, s).wait_recv()
            acc[here] += jnp.dot(corner[k, here], ops[2], preferred_element_type=jnp.float32)

        for c in range(width // batches):
            cut = pl.ds(c * batches, batches)
            traces[k + 1, here, cut] = jnp.where(
                start[here] <= k, acc[here, cut], 0.0
            ).astype(jnp.bfloat16)

        @pl.when(k < last)
        def _():
            for g in groups:
                send(k + 1, g)

    def tick(k, carry):
        for kind, groups in ORDER:
            if kind == "late":
                pl.when(k > 1)(functools.partial(corner_part, k - 1, groups))
            else:
                dict(take=pass_on, dot=straight_part, end=corner_part)[kind](k, groups)
        return carry

    lax.fori_loop(1, TICKS, tick, 0)
    for kind, groups in ORDER:
        if kind == "late":
            corner_part(last, groups)
    out_ref[...] = traces[TICKS]

    def drain(k, carry):
        s = sign_of(k)
        for g in range(len(GROUPS)):
            route = routes(g, s)
            pl.when(route["up"])(lambda: up_copy(k, g, s).wait_send())
            pl.when(route["left"])(lambda: left_copy(k, g, s).wait_send())
            pl.when(route["diag"])(lambda: diag_copy(k, g, s).wait_send())
            pl.when(route["relay"])(lambda: relay_copy(k, g, s).wait_send())
            if g in VIA:
                pl.when(route["via"])(lambda: via_copy(k, g, s).wait_send())
                pl.when(route["passed"])(lambda: pass_copy(k, g, s).wait_send())
                pl.when(route["turned"])(lambda: turn_copy(k, g, s).wait_send())
        return carry

    lax.fori_loop(1, TICKS, drain, 0)


def body(rhs, operators, positions, start_tick):
    batches, width = rhs.shape[2:]
    n = len(GROUPS)
    sems = pltpu.SemaphoreType.DMA((TICKS, n))
    slots = pltpu.VMEM((TICKS, batches, width), jnp.bfloat16)
    vmem = pl.BlockSpec(memory_space=pltpu.VMEM)
    out = pl.pallas_call(
        sweep_kernel,
        out_shape=jax.ShapeDtypeStruct((batches, width), jnp.bfloat16),
        in_specs=[pl.BlockSpec(memory_space=pltpu.HBM)] * 4,
        out_specs=vmem,
        scratch_shapes=[
            pltpu.VMEM((batches, width), jnp.bfloat16),
            pltpu.VMEM((1, batches), jnp.int32),
            pltpu.VMEM((1, batches), jnp.int32),
            pltpu.VMEM((3, width, width), jnp.bfloat16),
            pltpu.VMEM((TICKS + 1, batches, width), jnp.bfloat16),
            slots, slots, slots, slots,
            pltpu.VMEM((batches, width), jnp.float32),
            pltpu.VMEM((batches, batches), jnp.int32),
            pltpu.VMEM((batches, width), jnp.float32),
            pltpu.SemaphoreType.DMA((3,)),
            pltpu.SemaphoreType.DMA((3,)),
            sems, sems, sems, sems, sems, sems, sems, sems, sems, sems, sems,
        ],
        compiler_params=pltpu.CompilerParams(
            collective_id=0, has_side_effects=True, vmem_limit_bytes=63 << 20
        ),
    )(rhs[0, 0], operators[0, 0], positions[None], start_tick[None])
    return out[None, None]


def solution(mesh):
    placed = (P("row", "col", None, None), P("row", "col", None, None, None), P(), P())
    return jax.shard_map(
        body, mesh=mesh, in_specs=placed, out_specs=P("row", "col", None, None), check_vma=False
    )
```

```python
import functools

import jax
import jax.numpy as jnp
from jax import lax
from jax.experimental import pallas as pl
from jax.experimental.pallas import tpu as pltpu
from jax.sharding import PartitionSpec as P

TICKS = 8
TURN = 4
GROUPS = (32,)*4
DIRECT_ON = ()
DIRECT_OFF = ()
VIA = (1,3)
VIA_ODD = (0,1,2,3)
HALF = 4
ORDER = (('take', (0,)), ('late', (3,)), ('take', (1,)), ('dot', (0, 1)), ('end', (0,)), ('take', (2,)), ('end', (1,)), ('take', (3,)), ('dot', (2, 3)), ('end', (2,)))


def sweep_kernel(
    rhs_hbm, ops_hbm, pos_hbm, start_hbm, out_ref,
    rhs_ref, pos_ref, start_ref, ops, traces, up, left, corner, via, source, start, acc,
    in_sem, op_sem, up_send, up_recv, left_send, left_recv, cor_send, cor_recv,
    via_send, via_recv, pass_send, turn_send, diag_send,
):
    row, col = lax.axis_index("row"), lax.axis_index("col")
    rows, cols = lax.axis_size("row"), lax.axis_size("col")
    batches, width = rhs_hbm.shape
    last = TICKS - 1

    def op_copy(n):
        return pltpu.make_async_copy(ops_hbm.at[n], ops.at[n], op_sem.at[n])

    small = [
        pltpu.make_async_copy(there, here, in_sem.at[n])
        for n, (there, here) in enumerate(
            ((rhs_hbm, rhs_ref), (pos_hbm, pos_ref), (start_hbm, start_ref))
        )
    ]

    def in_rows(r):
        return jnp.logical_and(r >= 0, r < rows)

    def in_cols(c):
        return jnp.logical_and(c >= 0, c < cols)

    partners = [(-1, 0), (1, 0), (0, -1), (0, 1)]
    partners += [(-1, -1), (1, 1)]
    slot = lax.rem(row, HALF)
    is_end = jnp.logical_or(slot == 0, slot == HALF - 1)
    other_end = jnp.where(slot == 0, row + HALF - 1, row - (HALF - 1))
    other_half = lax.rem(row + HALF, 2 * HALF)
    beside = col + jnp.where(row < HALF, 1, -1)

    barrier = pltpu.get_barrier_semaphore()

    def greet(r, c):
        pl.semaphore_signal(barrier, inc=1, device_id={"row": r, "col": c})

    for dr, dc in partners:
        @pl.when(jnp.logical_and(in_rows(row + dr), in_cols(col + dc)))
        def _(dr=dr, dc=dc):
            greet(row + dr, col + dc)

    @pl.when(is_end)
    def _():
        greet(other_end, col)
        greet(other_half, col)

    @pl.when(jnp.logical_and(is_end, in_cols(beside)))
    def _():
        greet(other_half, beside)

    for copy in small:
        copy.start()
    for n in range(3):
        op_copy(n).start()
    for copy in small:
        copy.wait()

    pos = jnp.broadcast_to(pos_ref[...], (batches, batches)).T
    first = jnp.broadcast_to(start_ref[...], (batches, batches)).T
    start[...] = first
    own = pos - (row * cols + col) * width
    lane = lax.broadcasted_iota(jnp.int32, (batches, batches), 1)
    for c in range(width // batches):
        cut = pl.ds(c * batches, batches)
        spike = jnp.where(own == lane + c * batches, 4.0, 0.0)
        value = rhs_ref[:, cut].astype(jnp.float32) + spike
        source[:, cut] = value
        traces[1, :, cut] = jnp.where(first <= 0, value, 0.0).astype(jnp.bfloat16)

    def sign_of(k):
        return jnp.where(k < TURN, 1, -1)

    def on_chip(c, s):
        return lax.rem(c, 2) == jnp.where(s > 0, 0, 1)

    def direct(c, s, g):
        on = on_chip(c, s)
        return jnp.logical_or(
            jnp.logical_and(on, g in DIRECT_ON), jnp.logical_and(jnp.logical_not(on), g in DIRECT_OFF)
        )

    bounds = []
    at = 0
    for size in GROUPS:
        bounds.append((at, size))
        at += size

    def remote(src, dst, send, recv, r, c):
        return pltpu.make_async_remote_copy(
            src, dst, send, recv, device_id={"row": r, "col": c},
            device_id_type=pl.DeviceIdType.MESH,
        )

    def up_copy(k, g, s):
        a, n = bounds[g]
        return remote(traces.at[k, pl.ds(a, n)], up.at[k, pl.ds(a, n)],
                      up_send.at[k, g], up_recv.at[k, g], row + s, col)

    def left_copy(k, g, s):
        a, n = bounds[g]
        return remote(traces.at[k, pl.ds(a, n)], left.at[k, pl.ds(a, n)],
                      left_send.at[k, g], left_recv.at[k, g], row, col + s)

    def diag_copy(k, g, s):
        a, n = bounds[g]
        return remote(traces.at[k, pl.ds(a, n)], corner.at[k, pl.ds(a, n)],
                      diag_send.at[k, g], cor_recv.at[k, g], row + s, col + s)

    def relay_copy(k, g, s):
        a, n = bounds[g]
        return remote(up.at[k, pl.ds(a, n)], corner.at[k, pl.ds(a, n)],
                      cor_send.at[k, g], cor_recv.at[k, g], row, col + s)

    def via_copy(k, g, s):
        a, n = bounds[g]
        return remote(traces.at[k, pl.ds(a, n)], via.at[k, pl.ds(a, n)],
                      via_send.at[k, g], via_recv.at[k, g], other_end, col)

    def pass_copy(k, g, s):
        a, n = bounds[g]
        return remote(via.at[k, pl.ds(a, n)], up.at[k, pl.ds(a, n)],
                      pass_send.at[k, g], up_recv.at[k, g], other_half, col)

    def turn_copy(k, g, s):
        a, n = bounds[g]
        return remote(via.at[k, pl.ds(a, n)], corner.at[k, pl.ds(a, n)],
                      turn_send.at[k, g], cor_recv.at[k, g], other_half, col + s)

    def both(a, b):
        return jnp.logical_and(a, b)

    def crosses(s):
        return row == jnp.where(s > 0, HALF - 1, HALF)

    def enters(s):
        return row == jnp.where(s > 0, HALF, HALF - 1)

    def passes(s):
        return row == jnp.where(s > 0, 0, 2 * HALF - 1)

    def routes(g, s):
        to_row, to_col, from_row = in_rows(row + s), in_cols(col + s), in_rows(row - s)
        straight = direct(col, s, g)
        off = jnp.logical_not(on_chip(col, s))
        to_diag = straight
        goes = jnp.where(lax.rem(col, 2) == 0, g in VIA, g in VIA_ODD)
        leaps = both(crosses(s), goes)
        to_row_now = both(to_row, jnp.logical_not(leaps))
        to_diag = jnp.logical_or(
            both(to_diag, jnp.logical_not(both(off, leaps))),
            both(both(off, crosses(s)), jnp.logical_not(goes)),
        )
        bent = both(off, enters(s))
        return dict(
            up=to_row_now,
            left=to_col,
            diag=both(both(to_row, to_col), to_diag),
            relay=both(both(from_row, to_col), jnp.logical_not(jnp.logical_or(straight, bent))),
            via=leaps,
            passed=both(passes(s), goes),
            turned=both(both(both(passes(s), to_col), off), goes),
        )

    def send(k, g):
        s = sign_of(k)
        route = routes(g, s)
        pl.when(route["up"])(lambda: up_copy(k, g, s).start())
        if g in VIA + VIA_ODD:
            pl.when(route["via"])(lambda: via_copy(k, g, s).start())
        pl.when(route["diag"])(lambda: diag_copy(k, g, s).start())
        pl.when(route["left"])(lambda: left_copy(k, g, s).start())

    peers = jnp.where(is_end, 2, 0) + jnp.where(jnp.logical_and(is_end, in_cols(beside)), 1, 0)
    for dr, dc in partners:
        peers += jnp.where(jnp.logical_and(in_rows(row + dr), in_cols(col + dc)), 1, 0)
    pl.semaphore_wait(barrier, peers)

    for g in range(len(GROUPS)):
        send(1, g)
    for n in range(3):
        op_copy(n).wait()

    def joined(groups):
        first, size = bounds[groups[0]][0], sum(bounds[g][1] for g in groups)
        return pl.ds(first, size)

    def pass_on(k, groups):
        s = sign_of(k)
        for g in groups:
            route = routes(g, s)
            if g in VIA + VIA_ODD:
                @pl.when(route["passed"])
                def _(g=g, route=route):
                    via_copy(k, g, s).wait_recv()
                    pl.when(route["turned"])(lambda: turn_copy(k, g, s).start())
                    pass_copy(k, g, s).start()

            @pl.when(in_rows(row - s))
            def _(g=g, route=route):
                up_copy(k, g, s).wait_recv()
                pl.when(route["relay"])(lambda: relay_copy(k, g, s).start())

    def straight_part(k, groups):
        s = sign_of(k)
        here = joined(groups)
        acc[here] = source[here]

        @pl.when(in_cols(col - s))
        def _():
            for g in groups:
                left_copy(k, g, s).wait_recv()
            acc[here] += jnp.dot(left[k, here], ops[1], preferred_element_type=jnp.float32)

        @pl.when(in_rows(row - s))
        def _():
            acc[here] += jnp.dot(up[k, here], ops[0], preferred_element_type=jnp.float32)

    def corner_part(k, groups):
        s = sign_of(k)
        here = joined(groups)

        @pl.when(jnp.logical_and(in_rows(row - s), in_cols(col - s)))
        def _():
            for g in groups:
                diag_copy(k, g, s).wait_recv()
            acc[here] += jnp.dot(corner[k, here], ops[2], preferred_element_type=jnp.float32)

        for c in range(width // batches):
            cut = pl.ds(c * batches, batches)
            traces[k + 1, here, cut] = jnp.where(
                start[here] <= k, acc[here, cut], 0.0
            ).astype(jnp.bfloat16)

        @pl.when(k < last)
        def _():
            for g in groups:
                send(k + 1, g)

    def tick(k, carry):
        for kind, groups in ORDER:
            if kind == "late":
                pl.when(k > 1)(functools.partial(corner_part, k - 1, groups))
            else:
                dict(take=pass_on, dot=straight_part, end=corner_part)[kind](k, groups)
        return carry

    lax.fori_loop(1, TICKS, tick, 0)
    for kind, groups in ORDER:
        if kind == "late":
            corner_part(last, groups)
    out_ref[...] = traces[TICKS]

    def drain(k, carry):
        s = sign_of(k)
        for g in range(len(GROUPS)):
            route = routes(g, s)
            pl.when(route["up"])(lambda: up_copy(k, g, s).wait_send())
            pl.when(route["left"])(lambda: left_copy(k, g, s).wait_send())
            pl.when(route["diag"])(lambda: diag_copy(k, g, s).wait_send())
            pl.when(route["relay"])(lambda: relay_copy(k, g, s).wait_send())
            if g in VIA + VIA_ODD:
                pl.when(route["via"])(lambda: via_copy(k, g, s).wait_send())
                pl.when(route["passed"])(lambda: pass_copy(k, g, s).wait_send())
                pl.when(route["turned"])(lambda: turn_copy(k, g, s).wait_send())
        return carry

    lax.fori_loop(1, TICKS, drain, 0)


def body(rhs, operators, positions, start_tick):
    batches, width = rhs.shape[2:]
    n = len(GROUPS)
    sems = pltpu.SemaphoreType.DMA((TICKS, n))
    slots = pltpu.VMEM((TICKS, batches, width), jnp.bfloat16)
    vmem = pl.BlockSpec(memory_space=pltpu.VMEM)
    out = pl.pallas_call(
        sweep_kernel,
        out_shape=jax.ShapeDtypeStruct((batches, width), jnp.bfloat16),
        in_specs=[pl.BlockSpec(memory_space=pltpu.HBM)] * 4,
        out_specs=vmem,
        scratch_shapes=[
            pltpu.VMEM((batches, width), jnp.bfloat16),
            pltpu.VMEM((1, batches), jnp.int32),
            pltpu.VMEM((1, batches), jnp.int32),
            pltpu.VMEM((3, width, width), jnp.bfloat16),
            pltpu.VMEM((TICKS + 1, batches, width), jnp.bfloat16),
            slots, slots, slots, slots,
            pltpu.VMEM((batches, width), jnp.float32),
            pltpu.VMEM((batches, batches), jnp.int32),
            pltpu.VMEM((batches, width), jnp.float32),
            pltpu.SemaphoreType.DMA((3,)),
            pltpu.SemaphoreType.DMA((3,)),
            sems, sems, sems, sems, sems, sems, sems, sems, sems, sems, sems,
        ],
        compiler_params=pltpu.CompilerParams(
            collective_id=0, has_side_effects=True, vmem_limit_bytes=63 << 20
        ),
    )(rhs[0, 0], operators[0, 0], positions[None], start_tick[None])
    return out[None, None]


def solution(mesh):
    placed = (P("row", "col", None, None), P("row", "col", None, None, None), P(), P())
    return jax.shard_map(
        body, mesh=mesh, in_specs=placed, out_specs=P("row", "col", None, None), check_vma=False
    )
```

```python
import functools

import jax
import jax.numpy as jnp
from jax import lax
from jax.experimental import pallas as pl
from jax.experimental.pallas import tpu as pltpu
from jax.sharding import PartitionSpec as P

TICKS = 8
TURN = 4
GROUPS = (32,)*4
DIRECT_ON = ()
DIRECT_OFF = ()
VIA = (1,3)
VIA_ODD = (0,1,2,3)
HALF = 4
ORDER = (('take', (0,)), ('late', (3,)), ('take', (1,)), ('dot', (0, 1)), ('end', (0,)), ('take', (2,)), ('end', (1,)), ('take', (3,)), ('dot', (2, 3)), ('end', (2,)))


def sweep_kernel(
    rhs_hbm, ops_hbm, pos_hbm, start_hbm, out_ref,
    rhs_ref, pos_ref, start_ref, ops, traces, up, left, corner, via, source, start, acc,
    in_sem, op_sem, up_send, up_recv, left_send, left_recv, cor_send, cor_recv,
    via_send, via_recv, pass_send, turn_send, diag_send,
):
    row, col = lax.axis_index("row"), lax.axis_index("col")
    rows, cols = lax.axis_size("row"), lax.axis_size("col")
    batches, width = rhs_hbm.shape
    last = TICKS - 1

    def op_copy(n):
        return pltpu.make_async_copy(ops_hbm.at[n], ops.at[n], op_sem.at[n])

    small = [
        pltpu.make_async_copy(there, here, in_sem.at[n])
        for n, (there, here) in enumerate(
            ((rhs_hbm, rhs_ref), (pos_hbm, pos_ref), (start_hbm, start_ref))
        )
    ]

    def in_rows(r):
        return jnp.logical_and(r >= 0, r < rows)

    def in_cols(c):
        return jnp.logical_and(c >= 0, c < cols)

    partners = [(-1, 0), (1, 0), (0, -1), (0, 1)]
    partners += [(-1, -1), (1, 1)]
    slot = lax.rem(row, HALF)
    is_end = jnp.logical_or(slot == 0, slot == HALF - 1)
    other_end = jnp.where(slot == 0, row + HALF - 1, row - (HALF - 1))
    other_half = lax.rem(row + HALF, 2 * HALF)
    beside = col + jnp.where(row < HALF, 1, -1)

    barrier = pltpu.get_barrier_semaphore()

    def greet(r, c):
        pl.semaphore_signal(barrier, inc=1, device_id={"row": r, "col": c})

    for dr, dc in partners:
        @pl.when(jnp.logical_and(in_rows(row + dr), in_cols(col + dc)))
        def _(dr=dr, dc=dc):
            greet(row + dr, col + dc)

    @pl.when(is_end)
    def _():
        greet(other_end, col)
        greet(other_half, col)

    @pl.when(jnp.logical_and(is_end, in_cols(beside)))
    def _():
        greet(other_half, beside)

    for copy in small:
        copy.start()
    for n in range(3):
        op_copy(n).start()
    for copy in small:
        copy.wait()

    pos = jnp.broadcast_to(pos_ref[...], (batches, batches)).T
    first = jnp.broadcast_to(start_ref[...], (batches, batches)).T
    start[...] = first
    own = pos - (row * cols + col) * width
    lane = lax.broadcasted_iota(jnp.int32, (batches, batches), 1)
    for c in range(width // batches):
        cut = pl.ds(c * batches, batches)
        spike = jnp.where(own == lane + c * batches, 4.0, 0.0)
        value = rhs_ref[:, cut].astype(jnp.float32) + spike
        source[:, cut] = value
        traces[1, :, cut] = jnp.where(first <= 0, value, 0.0).astype(jnp.bfloat16)

    def sign_of(k):
        return jnp.where(k < TURN, 1, -1)

    def on_chip(c, s):
        return lax.rem(c, 2) == jnp.where(s > 0, 0, 1)

    def direct(c, s, g):
        on = on_chip(c, s)
        return jnp.logical_or(
            jnp.logical_and(on, g in DIRECT_ON), jnp.logical_and(jnp.logical_not(on), g in DIRECT_OFF)
        )

    bounds = []
    at = 0
    for size in GROUPS:
        bounds.append((at, size))
        at += size

    def remote(src, dst, send, recv, r, c):
        return pltpu.make_async_remote_copy(
            src, dst, send, recv, device_id={"row": r, "col": c},
            device_id_type=pl.DeviceIdType.MESH,
        )

    def up_copy(k, g, s):
        a, n = bounds[g]
        return remote(traces.at[k, pl.ds(a, n)], up.at[k, pl.ds(a, n)],
                      up_send.at[k, g], up_recv.at[k, g], row + s, col)

    def left_copy(k, g, s):
        a, n = bounds[g]
        return remote(traces.at[k, pl.ds(a, n)], left.at[k, pl.ds(a, n)],
                      left_send.at[k, g], left_recv.at[k, g], row, col + s)

    def diag_copy(k, g, s):
        a, n = bounds[g]
        return remote(traces.at[k, pl.ds(a, n)], corner.at[k, pl.ds(a, n)],
                      diag_send.at[k, g], cor_recv.at[k, g], row + s, col + s)

    def relay_copy(k, g, s):
        a, n = bounds[g]
        return remote(up.at[k, pl.ds(a, n)], corner.at[k, pl.ds(a, n)],
                      cor_send.at[k, g], cor_recv.at[k, g], row, col + s)

    def via_copy(k, g, s):
        a, n = bounds[g]
        return remote(traces.at[k, pl.ds(a, n)], via.at[k, pl.ds(a, n)],
                      via_send.at[k, g], via_recv.at[k, g], other_end, col)

    def pass_copy(k, g, s):
        a, n = bounds[g]
        return remote(via.at[k, pl.ds(a, n)], up.at[k, pl.ds(a, n)],
                      pass_send.at[k, g], up_recv.at[k, g], other_half, col)

    def turn_copy(k, g, s):
        a, n = bounds[g]
        return remote(via.at[k, pl.ds(a, n)], corner.at[k, pl.ds(a, n)],
                      turn_send.at[k, g], cor_recv.at[k, g], other_half, col + s)

    def both(a, b):
        return jnp.logical_and(a, b)

    def crosses(s):
        return row == jnp.where(s > 0, HALF - 1, HALF)

    def enters(s):
        return row == jnp.where(s > 0, HALF, HALF - 1)

    def passes(s):
        return row == jnp.where(s > 0, 0, 2 * HALF - 1)

    def routes(g, s):
        to_row, to_col, from_row = in_rows(row + s), in_cols(col + s), in_rows(row - s)
        straight = direct(col, s, g)
        off = jnp.logical_not(on_chip(col, s))
        to_diag = straight
        goes = jnp.where(lax.rem(col, 2) == 0, g in VIA, g in VIA_ODD)
        leaps = both(crosses(s), goes)
        to_row_now = both(to_row, jnp.logical_not(leaps))
        to_diag = jnp.logical_or(
            both(to_diag, jnp.logical_not(both(off, leaps))),
            both(both(off, crosses(s)), jnp.logical_not(goes)),
        )
        bent = both(off, enters(s))
        return dict(
            up=to_row_now,
            left=to_col,
            diag=both(both(to_row, to_col), to_diag),
            relay=both(both(from_row, to_col), jnp.logical_not(jnp.logical_or(straight, bent))),
            via=leaps,
            passed=both(passes(s), goes),
            turned=both(both(both(passes(s), to_col), off), goes),
        )

    def send(k, g):
        s = sign_of(k)
        route = routes(g, s)
        pl.when(route["left"])(lambda: left_copy(k, g, s).start())
        pl.when(route["up"])(lambda: up_copy(k, g, s).start())
        if g in VIA + VIA_ODD:
            pl.when(route["via"])(lambda: via_copy(k, g, s).start())
        pl.when(route["diag"])(lambda: diag_copy(k, g, s).start())

    peers = jnp.where(is_end, 2, 0) + jnp.where(jnp.logical_and(is_end, in_cols(beside)), 1, 0)
    for dr, dc in partners:
        peers += jnp.where(jnp.logical_and(in_rows(row + dr), in_cols(col + dc)), 1, 0)
    pl.semaphore_wait(barrier, peers)

    for g in range(len(GROUPS)):
        send(1, g)
    for n in range(3):
        op_copy(n).wait()

    def joined(groups):
        first, size = bounds[groups[0]][0], sum(bounds[g][1] for g in groups)
        return pl.ds(first, size)

    def pass_on(k, groups):
        s = sign_of(k)
        for g in groups:
            route = routes(g, s)
            if g in VIA + VIA_ODD:
                @pl.when(route["passed"])
                def _(g=g, route=route):
                    via_copy(k, g, s).wait_recv()
                    pl.when(route["turned"])(lambda: turn_copy(k, g, s).start())
                    pass_copy(k, g, s).start()

            @pl.when(in_rows(row - s))
            def _(g=g, route=route):
                up_copy(k, g, s).wait_recv()
                pl.when(route["relay"])(lambda: relay_copy(k, g, s).start())

    def straight_part(k, groups):
        s = sign_of(k)
        here = joined(groups)
        acc[here] = source[here]

        @pl.when(in_cols(col - s))
        def _():
            for g in groups:
                left_copy(k, g, s).wait_recv()
            acc[here] += jnp.dot(left[k, here], ops[1], preferred_element_type=jnp.float32)

        @pl.when(in_rows(row - s))
        def _():
            acc[here] += jnp.dot(up[k, here], ops[0], preferred_element_type=jnp.float32)

    def corner_part(k, groups):
        s = sign_of(k)
        here = joined(groups)

        @pl.when(jnp.logical_and(in_rows(row - s), in_cols(col - s)))
        def _():
            for g in groups:
                diag_copy(k, g, s).wait_recv()
            acc[here] += jnp.dot(corner[k, here], ops[2], preferred_element_type=jnp.float32)

        for c in range(width // batches):
            cut = pl.ds(c * batches, batches)
            traces[k + 1, here, cut] = jnp.where(
                start[here] <= k, acc[here, cut], 0.0
            ).astype(jnp.bfloat16)

        @pl.when(k < last)
        def _():
            for g in groups:
                send(k + 1, g)

    def tick(k, carry):
        for kind, groups in ORDER:
            if kind == "late":
                pl.when(k > 1)(functools.partial(corner_part, k - 1, groups))
            else:
                dict(take=pass_on, dot=straight_part, end=corner_part)[kind](k, groups)
        return carry

    lax.fori_loop(1, TICKS, tick, 0)
    for kind, groups in ORDER:
        if kind == "late":
            corner_part(last, groups)
    out_ref[...] = traces[TICKS]

    def drain(k, carry):
        s = sign_of(k)
        for g in range(len(GROUPS)):
            route = routes(g, s)
            pl.when(route["up"])(lambda: up_copy(k, g, s).wait_send())
            pl.when(route["left"])(lambda: left_copy(k, g, s).wait_send())
            pl.when(route["diag"])(lambda: diag_copy(k, g, s).wait_send())
            pl.when(route["relay"])(lambda: relay_copy(k, g, s).wait_send())
            if g in VIA + VIA_ODD:
                pl.when(route["via"])(lambda: via_copy(k, g, s).wait_send())
                pl.when(route["passed"])(lambda: pass_copy(k, g, s).wait_send())
                pl.when(route["turned"])(lambda: turn_copy(k, g, s).wait_send())
        return carry

    lax.fori_loop(1, TICKS, drain, 0)


def body(rhs, operators, positions, start_tick):
    batches, width = rhs.shape[2:]
    n = len(GROUPS)
    sems = pltpu.SemaphoreType.DMA((TICKS, n))
    slots = pltpu.VMEM((TICKS, batches, width), jnp.bfloat16)
    vmem = pl.BlockSpec(memory_space=pltpu.VMEM)
    out = pl.pallas_call(
        sweep_kernel,
        out_shape=jax.ShapeDtypeStruct((batches, width), jnp.bfloat16),
        in_specs=[pl.BlockSpec(memory_space=pltpu.HBM)] * 4,
        out_specs=vmem,
        scratch_shapes=[
            pltpu.VMEM((batches, width), jnp.bfloat16),
            pltpu.VMEM((1, batches), jnp.int32),
            pltpu.VMEM((1, batches), jnp.int32),
            pltpu.VMEM((3, width, width), jnp.bfloat16),
            pltpu.VMEM((TICKS + 1, batches, width), jnp.bfloat16),
            slots, slots, slots, slots,
            pltpu.VMEM((batches, width), jnp.float32),
            pltpu.VMEM((batches, batches), jnp.int32),
            pltpu.VMEM((batches, width), jnp.float32),
            pltpu.SemaphoreType.DMA((3,)),
            pltpu.SemaphoreType.DMA((3,)),
            sems, sems, sems, sems, sems, sems, sems, sems, sems, sems, sems,
        ],
        compiler_params=pltpu.CompilerParams(
            collective_id=0, has_side_effects=True, vmem_limit_bytes=63 << 20
        ),
    )(rhs[0, 0], operators[0, 0], positions[None], start_tick[None])
    return out[None, None]


def solution(mesh):
    placed = (P("row", "col", None, None), P("row", "col", None, None, None), P(), P())
    return jax.shard_map(
        body, mesh=mesh, in_specs=placed, out_specs=P("row", "col", None, None), check_vma=False
    )
```
